256 devices in a mesh: ed: 16 (over z, core), ep: 16 (over x, y).
Axes of the slice: x: 4, y: 4, z: 8, core: 2. Of those that a mesh axis runs over, the one named last changes fastest.
Arguments:
- grad_out: bfloat16 [14336, 4096], P(('ed', 'ep')), may hold values from -6 to 6
- routes: int32 [14336, 8], P(('ed', 'ep')), may hold values from 0 to 15, all different within a row; in each aligned block of 56 rows (0 to 55, 56 to 111, ...) at most 35 rows name the same one
- gates: bfloat16 [14336, 8], P(('ed', 'ep')), may hold values from 0.049804688 to 0.29882812
- hidden: bfloat16 [16, 16, 16, 35, 1536], P('ed', None, 'ep'), may hold values from -0.29882812 to 0.29882812
- master: float32 [16, 4096, 1536], P('ep', 'ed'), may hold values from -0.15625 to 0.15625
- moment_one: float32 [16, 4096, 1536], P('ep', 'ed'), may hold values from -3 to 3
- moment_two: float32 [16, 4096, 1536], P('ep', 'ed'), may hold values from 0.02 to 1
Outputs:
- grad_gates: float32 [14336, 8], P(('ed', 'ep'))
- grad_hidden: bfloat16 [16, 16, 16, 35, 1536], P('ed', None, 'ep')
- new_master: float32 [16, 4096, 1536], P('ep', 'ed')
- new_moment_one: float32 [16, 4096, 1536], P('ep', 'ed')
- new_moment_two: float32 [16, 4096, 1536], P('ep', 'ed')
The draws below stay inside these ranges and needn't reach their ends.
Inputs may be any that keep to these rules, and one draw needn't show every extreme that they name: `routes`: each row names 8 different experts; among the 56 rows of one device no expert is named by more than 35 rows, a bound that some block reaches.
All inputs are finite; a program needn't handle non-finite values.
Results may differ from the reference program's by a relative error of at most 0.008.
Values may be sent and summed in bfloat16 or wider, within the bound.
A program may use at most 192 MiB of HBM per device.

```python
import math
import jax
import jax.numpy as jnp
import numpy as np
from jax import lax

D = 4096
FF = 1536
TOK_DEV = 56
EXPERTS = 16
TOPK = 8
CAP = 35
TOKENS = 14336
N_ED = 16


def levels(own_key, extent, shards, least, largest):
    def one(position, parts):
        steps = jax.random.uniform(jax.random.fold_in(jax.random.fold_in(own_key, 6), position), (parts,), jnp.float32, least / len(shards), largest / len(shards))
        return jnp.repeat(jnp.exp(steps), extent[position] // parts).reshape((-1,) + (1,) * (len(extent) - position - 1))

    gain = one(*shards[0])
    for cut in shards[1:]:
        gain = gain * one(*cut)
    return gain


def routed_block(key, own, number, rows, number_of, top, most, lean):
    order = jax.random.permutation(key, number_of)
    crowded, common = load_shares(number_of, rows * top, most, lean, True), load_shares(number_of, rows * top, most, lean, False)
    places = jnp.arange(number_of)

    def named(tallies, turn):
        used = int((tallies > 0).sum())
        fixed = max(1, used // 4)
        moved = fixed + (places - fixed + turn * (used - fixed)) % max(1, number_of - fixed)
        return jnp.zeros((number_of,), jnp.int32).at[order[jnp.where(places < fixed, places, moved)]].set(jnp.asarray(tallies, jnp.int32))

    tallies = jnp.where(number % 4 == 0, named(crowded, number // 4), named(common, number - number // 4 - 1))
    mixed = jax.random.permutation(jax.random.fold_in(own, 3), number_of)
    donor, sink = mixed[0:number_of // 2 * 2:2], mixed[1:number_of // 2 * 2:2]
    slack = jnp.minimum(tallies[donor] - 1, most - tallies[sink]) // 2
    slack = jnp.where((donor == order[0]) | (sink == order[0]) | (tallies[sink] == 0), 0, jnp.maximum(slack, 0))
    moved = jax.random.randint(jax.random.fold_in(own, 4), (number_of // 2,), 0, 1 << 20) % (slack + 1)
    tallies = tallies.at[donor].add(-moved).at[sink].add(moved)
    items = jnp.searchsorted(jnp.cumsum(tallies), jnp.arange(rows * top), side="right").astype(jnp.int32)
    listing = items.reshape(top, rows).T
    listing = listing[jax.random.permutation(jax.random.fold_in(own, 1), rows)]
    turn = jax.random.randint(jax.random.fold_in(own, 2), (rows, 1), 0, top)
    return jnp.take_along_axis(listing, (jnp.arange(top)[None, :] + turn) % top, axis=1)


def load_shares(count, total, most, lean, full):
    weights = [(1 << 20) // math.isqrt(standing ** lean) + 1 for standing in range(1, count + 1)]
    largest = most if full else min(most, max(-(-total // count), total * weights[0] // sum(weights)))
    least = 1 if total - largest >= count - 1 else 0
    holding, surplus = [largest] + [least] * (count - 1), total - largest - least * (count - 1)
    while surplus > 0:
        free = [i for i in range(1, count) if holding[i] < largest] or [i for i in range(1, count) if holding[i] < most]
        mass, left = sum([weights[i] for i in free]), surplus
        for i in free:
            more = min(most - holding[i], max(1, left * weights[i] // mass), surplus)
            holding[i] = holding[i] + more
            surplus = surplus - more
    return np.array(holding)


def bell_draw(stream_key, shape, scale, limit, pieces=(), held_as=jnp.bfloat16):
    entries = scale * jax.random.normal(stream_key, shape, jnp.float32)
    if pieces:
        entries = entries * levels(stream_key, shape, pieces, -0.22, 0.18)
    return jnp.clip(entries, -limit, limit).astype(held_as)


def setup_inputs(seed: int = 0) -> dict:
    keys = jax.random.split(jax.random.key(seed), 8)
    grad_out = bell_draw(keys[0], (TOKENS, D), 1.0, 6.0, ((0, 256),))
    routes_keys = jax.random.split(jax.random.fold_in(keys[1], 1), TOKENS // TOK_DEV)
    routes_turns = jax.random.permutation(jax.random.fold_in(keys[1], 3), TOKENS // TOK_DEV)
    routes = jax.vmap(lambda own, number: routed_block(jax.random.fold_in(keys[1], 2), own, number, TOK_DEV, EXPERTS, TOPK, CAP, 2))(routes_keys, routes_turns).reshape((TOKENS, TOPK))
    gates = jnp.clip(0.049804688 + 0.24902344 * jax.random.uniform(keys[2], (TOKENS, TOPK), jnp.float32) ** levels(keys[2], (TOKENS, TOPK), ((0, 256),), -0.2, 0.2), 0.049804688, 0.29882812).astype(jnp.bfloat16)
    hidden = bell_draw(keys[3], (N_ED, EXPERTS, EXPERTS, CAP, FF), 0.05, 0.29882812, ((0, 16), (2, 16)))
    master = bell_draw(keys[4], (EXPERTS, D, FF), FF ** -0.5, 0.15625, ((0, 16), (1, 16)), jnp.float32)
    moment_one = bell_draw(keys[5], (EXPERTS, D, FF), 0.3, 3.0, ((0, 16), (1, 16)), jnp.float32)
    moment_two = jnp.clip(jnp.exp(math.log(1.0) - 3.912023 * jax.random.uniform(keys[6], (EXPERTS, D, FF), jnp.float32) ** levels(keys[6], (EXPERTS, D, FF), ((0, 16), (1, 16)), -0.2, 0.2)), 0.02, 1.0)
    return {"grad_out": grad_out, "routes": routes, "gates": gates, "hidden": hidden, "master": master, "moment_one": moment_one, "moment_two": moment_two}


beta_first = 0.9
beta_second = 0.95
learn_rate = 0.01
adam_eps = 1e-08

def slot_table(block_routes):
    flat_routes = block_routes.reshape(-1)
    onehot = (flat_routes[:, None] == jnp.arange(EXPERTS, dtype=jnp.int32)[None, :]).astype(jnp.int32)
    before = jnp.cumsum(onehot, axis=0) - onehot
    return lax.optimization_barrier(jnp.sum(before * onehot, axis=1)).astype(jnp.int32)

def place_block(block_grad, block_routes, block_gates):
    slot_index = slot_table(block_routes)
    flat_routes = block_routes.reshape(-1)
    token_index = jnp.repeat(jnp.arange(TOK_DEV, dtype=jnp.int32), TOPK)
    row_table = jnp.zeros((EXPERTS, CAP, D), jnp.bfloat16).at[flat_routes, slot_index].set(block_grad[token_index])
    gate_table = jnp.zeros((EXPERTS, CAP), jnp.bfloat16).at[flat_routes, slot_index].set(block_gates.reshape(-1))
    return (row_table, gate_table, slot_index)

def pick_block(prob_block, block_routes, slot_index):
    return prob_block[block_routes.reshape(-1), slot_index].reshape(TOK_DEV, TOPK)

def reference(grad_out, routes, gates, hidden, master, moment_one, moment_two):
    weights = lax.optimization_barrier(master.astype(jnp.bfloat16)).astype(jnp.float32)
    grad_blocks = grad_out.reshape(N_ED, EXPERTS, TOK_DEV, D)
    route_blocks = routes.reshape(N_ED, EXPERTS, TOK_DEV, TOPK)
    gate_blocks = gates.reshape(N_ED, EXPERTS, TOK_DEV, TOPK)

    def replica(grad_sum, inputs):
        block_grad, block_routes, block_gates, saved_rows = inputs
        grad_rows, gate_rows, slot_index = jax.vmap(place_block)(block_grad, block_routes, block_gates)
        rows_wide = grad_rows.astype(jnp.float32)
        saved_wide = saved_rows.astype(jnp.float32)
        upward = jnp.einsum('secd,edf->secf', rows_wide, weights)
        expert_output = jnp.einsum('secf,edf->secd', saved_wide, weights)
        prob_slot = lax.optimization_barrier(jnp.sum(rows_wide * expert_output, axis=3))
        grad_gates = jax.vmap(pick_block)(prob_slot, block_routes, slot_index)
        gate_wide = gate_rows.astype(jnp.float32)[..., None]
        grad_hidden = (gate_wide * upward).astype(jnp.bfloat16)
        weighted = lax.optimization_barrier((gate_wide * rows_wide).astype(jnp.bfloat16)).astype(jnp.float32)
        partial_grad = jnp.einsum('secd,secf->edf', weighted, saved_wide)
        partial_grad = lax.optimization_barrier(partial_grad.astype(jnp.bfloat16)).astype(jnp.float32)
        return (grad_sum + partial_grad, (grad_hidden, grad_gates))
    start_sum = jnp.zeros((EXPERTS, D, FF), jnp.float32)
    gradient, (grad_hidden, grad_gates) = lax.scan(replica, start_sum, (grad_blocks, route_blocks, gate_blocks, hidden))
    new_moment_one = beta_first * moment_one + (1.0 - beta_first) * gradient
    new_moment_two = beta_second * moment_two + (1.0 - beta_second) * gradient * gradient
    first_bias = 1.0 - beta_first ** 20
    second_bias = 1.0 - beta_second ** 20
    update = new_moment_one / first_bias / (jnp.sqrt(new_moment_two / second_bias) + adam_eps)
    new_master = master - learn_rate * update
    return (grad_gates.reshape(TOKENS, TOPK), grad_hidden, new_master, new_moment_one, new_moment_two)
```

```python
import jax
import jax.numpy as jnp
from jax import lax
from jax.experimental import pallas as pl
from jax.experimental.pallas import tpu as pltpu
from jax.sharding import PartitionSpec as P

beta_first = 0.9
beta_second = 0.95
learn_rate = 0.01
adam_eps = 1e-08

MESH = pl.DeviceIdType.MESH
BF = jnp.bfloat16
F32 = jnp.float32
I32 = jnp.int32

NZ = 8
SIDE = 4
EXP = 16
TOK = 56
ROWS = 64
ALL = EXP * ROWS
WIDTH = 4096
HID = 1536
HALF = HID // 2
CAP = 35
SLOTS = CAP * EXP
OWN = 256
COL = 256


def dot(a, b):
    return jnp.dot(a, b, preferred_element_type=F32)


def body(
    go_ref, routes_ref, gates_ref, hid_ref, master_ref,
    gh_ref, grad_ref, gg_ref,
    tok, wts, gd, tile, gatec, sel_t, h_tok, hg_t, acc, gmul, pown, stage, psib, rsb, prob, probr,
    xy_s, xy_r, zw_s, zw_r, sw_s, sw_r, gd_s, gd_r, ps_s, ps_r, rs_s, rs_r, pr_s, pr_r,
):
    ed = lax.axis_index("ed")
    ep = lax.axis_index("ep")
    z, c = ed // 2, ed % 2
    x, y = ep // SIDE, ep % SIDE

    def zdev(k):
        return {"ed": lax.rem(z + k + NZ, NZ) * 2 + c, "ep": ep}

    sibling = {"ed": z * 2 + 1 - c, "ep": ep}

    def peer(o):
        return lax.rem(ep + o, EXP)

    def send(src, dst, ssem, rsem, dev):
        copy = pltpu.make_async_remote_copy(
            src_ref=src, dst_ref=dst, send_sem=ssem, recv_sem=rsem,
            device_id=dev, device_id_type=MESH,
        )
        copy.start()

    def arrived(ref, rsem, ssem):
        pltpu.make_async_remote_copy(
            src_ref=ref, dst_ref=ref, send_sem=ssem, recv_sem=rsem,
            device_id=sibling, device_id_type=MESH,
        ).wait_recv()

    def sent(ref, ssem, rsem):
        pltpu.make_async_remote_copy(
            src_ref=ref, dst_ref=ref, send_sem=ssem, recv_sem=rsem,
            device_id=sibling, device_id_type=MESH,
        ).wait_send()

    barrier = pltpu.get_barrier_semaphore()

    def greet(o, carry):
        pl.semaphore_signal(barrier, inc=1, device_id={"ed": ed, "ep": peer(o)}, device_id_type=MESH)
        return carry

    lax.fori_loop(1, EXP, greet, 0)
    for dev in (zdev(1), zdev(-1), sibling):
        pl.semaphore_signal(barrier, inc=1, device_id=dev, device_id_type=MESH)

    wts[ed] = master_ref[...].astype(BF)
    for q in range(4):
        cols = pl.ds(q * 1024, 1024)
        wide = go_ref[:, cols].astype(F32)
        tok[ep, :, cols] = jnp.concatenate([wide, jnp.zeros((ROWS - TOK, 1024), F32)], axis=0).astype(BF)
    expert_row = lax.broadcasted_iota(I32, (EXP, TOK), 0)
    dense = jnp.zeros((EXP, TOK), F32)
    named = jnp.zeros((EXP, TOK), F32)
    for k in range(routes_ref.shape[0]):
        hit = routes_ref[k : k + 1, :] == expert_row
        dense = dense + jnp.where(hit, gates_ref[k : k + 1, :].astype(F32), 0.0)
        named = named + jnp.where(hit, 1.0, 0.0)
    tile[...] = jnp.zeros_like(tile)
    tile[0:EXP, 0:TOK] = dense
    tile[EXP : 2 * EXP, 0:TOK] = named
    table = jnp.transpose(tile[...])[0:ROWS, :]
    earlier = jnp.where(
        lax.broadcasted_iota(I32, (ROWS, ROWS), 1) < lax.broadcasted_iota(I32, (ROWS, ROWS), 0), 1.0, 0.0
    ).astype(BF)
    lane = lax.broadcasted_iota(I32, (ROWS, 128), 1)
    slot = dot(earlier, table.astype(BF))
    slot = jnp.where(table > 0.5, slot, -1.0)
    gd[ep] = jnp.where((lane >= EXP) & (lane < 2 * EXP), slot, table).astype(BF)

    pl.semaphore_wait(barrier, EXP - 1 + 3)

    streams = (("x", 1), ("x", -1), ("y", 1), ("y", -1))

    def block_of(q, da, db):
        first, sign = streams[q]
        a, b = (x, y) if first == "x" else (y, x)
        a = lax.rem(a - sign * da + SIDE, SIDE)
        b = lax.rem(b - sign * db + SIDE, SIDE)
        return a * SIDE + b if first == "x" else b * SIDE + a

    def piece(q, da, db):
        return tok.at[block_of(q, da, db), pl.ds(q * 16, 16), :]

    def line_dev(q, phase):
        first, sign = streams[q]
        along_x = (first == "x") == (phase == 1)
        nx = lax.rem(x + sign + SIDE, SIDE) if along_x else x
        ny = y if along_x else lax.rem(y + sign + SIDE, SIDE)
        return {"ed": ed, "ep": nx * SIDE + ny}

    def xy_send1(q, j):
        ref = piece(q, j, 0)
        send(ref, ref, xy_s.at[q, j], xy_r.at[q, j], line_dev(q, 1))

    def xy_send2(q, j, i):
        m = 3 + 4 * j + i
        ref = piece(q, i, j)
        send(ref, ref, xy_s.at[q, m], xy_r.at[q, m], line_dev(q, 2))

    def xy_step(n):
        for q in range(4):
            if n < 3:
                arrived(piece(q, n + 1, 0), xy_r.at[q, n], xy_s.at[q, n])
                if n < 2:
                    xy_send1(q, n + 1)
                xy_send2(q, 0, n + 1)
            else:
                j, i = (n - 3) // 4, (n - 3) % 4
                arrived(piece(q, i, j + 1), xy_r.at[q, n], xy_s.at[q, n])
                if j < 2:
                    xy_send2(q, j + 1, i)

    def wpiece(d, k, core):
        zo = lax.rem(z - k + NZ, NZ) if d == 0 else lax.rem(z + k, NZ)
        return wts.at[zo * 2 + core, pl.ds(d * 128, 128), :]

    def w_pass(k):
        for d in range(2):
            ref = wpiece(d, k, c)
            if k > 0:
                arrived(ref, zw_r.at[d, k - 1], zw_s.at[d, k - 1])
            if k < NZ - 1:
                send(ref, ref, zw_s.at[d, k], zw_r.at[d, k], zdev(1 if d == 0 else -1))
            send(ref, ref, sw_s.at[d, k], sw_r.at[d, k], sibling)

    def gd_send(o, carry):
        send(gd.at[ep], gd.at[ep], gd_s.at[o], gd_r.at[o], {"ed": ed, "ep": peer(o)})
        return carry

    lax.fori_loop(1, EXP, gd_send, 0)
    for q in range(4):
        xy_send1(q, 0)
    w_pass(0)
    for q in range(4):
        xy_send2(q, 0, 0)

    def gd_wait(o, carry):
        arrived(gd.at[peer(EXP - o)], gd_r.at[o], gd_s.at[o])
        return carry

    lax.fori_loop(1, EXP, gd_wait, 0)

    def choose(r):
        rows = pl.ds(r * 256, 256)
        mine = gd[4 * r : 4 * r + 4].reshape(256, 128).astype(F32)
        lanes = lax.broadcasted_iota(I32, (256, 128), 1)
        gate = jnp.sum(jnp.where(lanes == ep, mine, 0.0), axis=1, keepdims=True)
        place = jnp.sum(jnp.where(lanes == EXP + ep, mine, 0.0), axis=1, keepdims=True)
        source = (lax.broadcasted_iota(I32, (256, 1), 0) // ROWS + 4 * r).astype(F32)
        target = jnp.where(place >= 0.0, place * EXP + source, -1.0)
        gatec[rows, :] = jnp.broadcast_to(gate, (256, 128))
        turned = jnp.transpose(jnp.where(lanes == 0, target, jnp.where(lanes == 1, gate, 0.0)))
        slots_down = lax.broadcasted_iota(I32, (SLOTS, 256), 0).astype(F32)
        same = slots_down == turned[0:1, :]
        sel_t[:, rows] = jnp.where(same, 1.0, 0.0).astype(BF)
        gated = jnp.where(same, turned[1:2, :], 0.0).astype(BF)
        for f in range(3):
            cols = pl.ds(f * 512, 512)
            hg_t[cols, rows] = lax.dot_general(
                hid_ref[:, cols], gated, (((0,), (0,)), ((), ())), preferred_element_type=F32
            ).astype(BF)
        slots_across = lax.broadcasted_iota(I32, (256, SLOTS), 1).astype(F32)
        picked = jnp.where(slots_across == target, 1.0, 0.0).astype(BF)
        h_tok[rows, :] = dot(picked, hid_ref[...]).astype(BF)

    def p_compute(k, settled):
        place = lax.rem(k, 2)
        for d in range(2):
            zo = lax.rem(z - 1 - k + 2 * NZ, NZ) if d == 0 else lax.rem(z + 1 + k, NZ)
            left = hg_t[d * HALF : (d + 1) * HALF, :]

            def side(core):
                cols = pl.ds(pl.multiple_of((zo * 2 + core) * OWN, OWN), OWN)
                return tok[:, :, cols].reshape(ALL, OWN)

            if settled:
                sent(stage.at[d, place], ps_s.at[d, k - 2], ps_r.at[d, k - 2])
            stage[d, place] = dot(left, side(1 - c)).astype(BF)
            send(stage.at[d, place], psib.at[d, k], ps_s.at[d, k], ps_r.at[d, k], sibling)
            pown[d, place] = dot(left, side(c))

    def rs_step(k, first):
        place = lax.rem(k, 2)
        for d in range(2):
            arrived(psib.at[d, k], ps_r.at[d, k], ps_s.at[d, k])
            total = pown[d, place] + psib[d, k].astype(F32)
            if not first:
                arrived(rsb.at[d, k], rs_r.at[d, k - 1], rs_s.at[d, k - 1])
                total = total + rsb[d, k].astype(F32)
            rsb[d, k] = total.astype(BF)
            send(rsb.at[d, k], rsb.at[d, k + 1], rs_s.at[d, k], rs_r.at[d, k], zdev(1 if d == 0 else -1))

    def up_part(n):
        cols = pl.ds(pl.multiple_of(n * COL, COL), COL)
        acc[...] = jnp.zeros_like(acc)

        def deep(kk, carry):
            t = tok[:, :, pl.ds(pl.multiple_of(kk * 512, 512), 512)].reshape(ALL, 512)
            w = wts[pl.ds(kk * 2, 2), :, cols].reshape(512, COL)
            acc[...] += dot(t, w)
            return carry

        lax.fori_loop(0, WIDTH // 512, deep, 0)

        def finish(r, carry):
            rows = pl.ds(pl.multiple_of(r * 256, 256), 256)
            up = acc[rows, :]
            prod = up * h_tok[rows, cols].astype(F32)
            prob[rows, :] += prod[:, 0:128] + prod[:, 128:256]
            gate = gatec[rows, :]
            gmul[rows, :] = (jnp.concatenate([gate, gate], axis=1) * up).astype(BF)
            return carry

        lax.fori_loop(0, ALL // 256, finish, 0)
        gh_ref[:, cols] = dot(sel_t[...], gmul[...]).astype(BF)

    prob[...] = jnp.zeros_like(prob)
    xy_step(0)
    choose(0)
    xy_step(1)
    w_pass(1)
    choose(1)
    xy_step(2)
    xy_step(3)
    choose(2)
    xy_step(4)
    w_pass(2)
    choose(3)
    xy_step(5)
    xy_step(6)
    xy_step(7)
    w_pass(3)
    xy_step(8)
    xy_step(9)
    xy_step(10)
    w_pass(4)
    xy_step(11)
    xy_step(12)
    xy_step(13)
    w_pass(5)
    xy_step(14)
    p_compute(0, False)
    w_pass(6)
    p_compute(1, False)
    rs_step(0, True)
    w_pass(7)
    for k in range(NZ):
        for d in range(2):
            arrived(wpiece(d, k, 1 - c), sw_r.at[d, k], sw_s.at[d, k])

    def main(k, carry):
        p_compute(k + 1, True)
        up_part(k - 1)
        rs_step(k, False)
        return carry

    lax.fori_loop(1, NZ - 1, main, 0)

    for r in range(4):
        rows = pl.ds(r * 256, 256)
        prob[rows, :] = jnp.broadcast_to(jnp.sum(prob[rows, :], axis=1, keepdims=True), (256, 128))

    def prob_at(s):
        return prob.at[pl.ds(pl.multiple_of(s * ROWS, ROWS), ROWS), :]

    def pr_send(o, carry):
        send(prob_at(peer(o)), probr.at[ep], pr_s.at[o], pr_r.at[o], {"ed": ed, "ep": peer(o)})
        return carry

    lax.fori_loop(1, EXP, pr_send, 0)
    probr[ep] = prob[pl.ds(pl.multiple_of(ep * ROWS, ROWS), ROWS), :]

    for d in range(2):
        arrived(psib.at[d, NZ - 1], ps_r.at[d, NZ - 1], ps_s.at[d, NZ - 1])
        arrived(rsb.at[d, NZ - 1], rs_r.at[d, NZ - 2], rs_s.at[d, NZ - 2])
        total = pown[d, (NZ - 1) % 2] + psib[d, NZ - 1].astype(F32) + rsb[d, NZ - 1].astype(F32)
        grad_ref[:, d * HALF : (d + 1) * HALF] = jnp.transpose(total)

    def pr_wait(o, carry):
        arrived(probr.at[peer(EXP - o)], pr_r.at[o], pr_s.at[o])
        return carry

    lax.fori_loop(1, EXP, pr_wait, 0)
    lanes = lax.broadcasted_iota(I32, (ROWS, 128), 1)
    spread = jnp.zeros((ROWS, 128), F32)
    for e in range(EXP):
        spread = jnp.where(lanes == e, probr[e], spread)
    tile[0:ROWS, :] = spread
    turned = jnp.transpose(tile[...])
    picked = jnp.zeros((routes_ref.shape[0], TOK), F32)
    for e in range(EXP):
        picked = picked + jnp.where(routes_ref[...] == e, turned[e : e + 1, 0:TOK], 0.0)
    gg_ref[...] = picked

    for q in range(4):
        for n in range(15):
            da, db = (n, 0) if n < 3 else ((n - 3) % 4, (n - 3) // 4)
            sent(piece(q, da, db), xy_s.at[q, n], xy_r.at[q, n])
    for d in range(2):
        for k in range(NZ):
            ref = wpiece(d, k, c)
            if k < NZ - 1:
                sent(ref, zw_s.at[d, k], zw_r.at[d, k])
                sent(rsb.at[d, k], rs_s.at[d, k], rs_r.at[d, k])
            sent(ref, sw_s.at[d, k], sw_r.at[d, k])
            if k >= NZ - 2:
                sent(stage.at[d, k % 2], ps_s.at[d, k], ps_r.at[d, k])

    def last(o, carry):
        sent(gd.at[ep], gd_s.at[o], gd_r.at[o])
        sent(prob_at(peer(o)), pr_s.at[o], pr_r.at[o])
        return carry

    lax.fori_loop(1, EXP, last, 0)


def local(grad_out, routes, gates, hidden, master, moment_one, moment_two):
    saved = jnp.transpose(hidden, (0, 2, 3, 1, 4)).reshape(SLOTS, HID)
    own = master.reshape(OWN, HID)
    vmem = pl.BlockSpec(memory_space=pltpu.VMEM)
    dma = pltpu.SemaphoreType.DMA
    gh, gradient, gg = pl.pallas_call(
        body,
        out_shape=(
            jax.ShapeDtypeStruct((SLOTS, HID), BF),
            jax.ShapeDtypeStruct((OWN, HID), F32),
            jax.ShapeDtypeStruct((routes.shape[1], TOK), F32),
        ),
        in_specs=[vmem] * 5,
        out_specs=(vmem,) * 3,
        scratch_shapes=[
            pltpu.VMEM((EXP, ROWS, WIDTH), BF),
            pltpu.VMEM((EXP, OWN, HID), BF),
            pltpu.VMEM((EXP, ROWS, 128), BF),
            pltpu.VMEM((128, 128), F32),
            pltpu.VMEM((ALL, 128), F32),
            pltpu.VMEM((SLOTS, ALL), BF),
            pltpu.VMEM((ALL, HID), BF),
            pltpu.VMEM((HID, ALL), BF),
            pltpu.VMEM((ALL, COL), F32),
            pltpu.VMEM((ALL, COL), BF),
            pltpu.VMEM((2, 2, HALF, OWN), F32),
            pltpu.VMEM((2, 2, HALF, OWN), BF),
            pltpu.VMEM((2, NZ, HALF, OWN), BF),
            pltpu.VMEM((2, NZ, HALF, OWN), BF),
            pltpu.VMEM((ALL, 128), F32),
            pltpu.VMEM((EXP, ROWS, 128), F32),
            dma((4, 15)), dma((4, 15)),
            dma((2, NZ - 1)), dma((2, NZ - 1)),
            dma((2, NZ)), dma((2, NZ)),
            dma((EXP,)), dma((EXP,)),
            dma((2, NZ)), dma((2, NZ)),
            dma((2, NZ - 1)), dma((2, NZ - 1)),
            dma((EXP,)), dma((EXP,)),
        ],
        compiler_params=pltpu.CompilerParams(
            collective_id=0, has_side_effects=True, vmem_limit_bytes=62 * 1024 * 1024
        ),
        cost_estimate=pl.CostEstimate(flops=25_000_000_000, bytes_accessed=8_000_000, transcendentals=0),
        name="expert_backward",
    )(grad_out, routes.T, gates.T, saved, own)

    gradient = gradient.reshape(master.shape)
    new_moment_one = beta_first * moment_one + (1.0 - beta_first) * gradient
    new_moment_two = beta_second * moment_two + (1.0 - beta_second) * gradient * gradient
    first_bias = 1.0 - beta_first**20
    second_bias = 1.0 - beta_second**20
    update = new_moment_one / first_bias / (jnp.sqrt(new_moment_two / second_bias) + adam_eps)
    new_master = master - learn_rate * update
    grad_hidden = jnp.transpose(gh.reshape(1, 1, CAP, EXP, HID), (0, 3, 1, 2, 4))
    return (gg.T, grad_hidden, new_master, new_moment_one, new_moment_two)


def solution(mesh):
    in_specs = (
        P(("ed", "ep"), None),
        P(("ed", "ep"), None),
        P(("ed", "ep"), None),
        P("ed", None, "ep", None, None),
        P("ep", "ed", None),
        P("ep", "ed", None),
        P("ep", "ed", None),
    )
    out_specs = (
        P(("ed", "ep"), None),
        P("ed", None, "ep", None, None),
        P("ep", "ed", None),
        P("ep", "ed", None),
        P("ep", "ed", None),
    )
    return jax.shard_map(local, mesh=mesh, in_specs=in_specs, out_specs=out_specs, check_vma=False)
```

```python
import jax
import jax.numpy as jnp
from jax import lax
from jax.experimental import pallas as pl
from jax.experimental.pallas import tpu as pltpu
from jax.sharding import PartitionSpec as P

beta_first = 0.9
beta_second = 0.95
learn_rate = 0.01
adam_eps = 1e-08

MESH = pl.DeviceIdType.MESH
BF = jnp.bfloat16
F32 = jnp.float32
I32 = jnp.int32

NZ = 8
SIDE = 4
EXP = 16
TOK = 56
ROWS = 64
ALL = EXP * ROWS
WIDTH = 4096
HID = 1536
HALF = HID // 2
CAP = 35
SLOTS = CAP * EXP
OWN = 256
COL = 256
LIMIT = 58
XY_PACE = 3.2
NSUB = 2
WSUB = OWN // NSUB
RSUB = HALF // NSUB


def dot(a, b):
    return jnp.dot(a, b, preferred_element_type=F32)


def body(
    go_ref, routes_ref, gates_ref, hid_hbm, master_hbm,
    gh_hbm, grad_hbm, gg_ref,
    tok, wts, gd, tile, gatec, sel_t, h_tok, hg_t, u, gmul, hid_ref, gh_part, pown, stage, psib, rsb, prob, probr,
    xy_s, xy_r, zw_s, zw_r, sw_s, sw_r, gd_s, gd_r, ps_s, ps_r, rs_s, rs_r, pr_s, pr_r, in_sem, gh_sem, grad_sem,
):
    ed = lax.axis_index("ed")
    ep = lax.axis_index("ep")
    z, c = ed // 2, ed % 2
    x, y = ep // SIDE, ep % SIDE

    def zdev(k):
        return {"ed": lax.rem(z + k + NZ, NZ) * 2 + c, "ep": ep}

    sibling = {"ed": z * 2 + 1 - c, "ep": ep}

    def peer(o):
        return lax.rem(ep + o, EXP)

    def send(src, dst, ssem, rsem, dev):
        copy = pltpu.make_async_remote_copy(
            src_ref=src, dst_ref=dst, send_sem=ssem, recv_sem=rsem,
            device_id=dev, device_id_type=MESH,
        )
        copy.start()

    def arrived(ref, rsem, ssem):
        pltpu.make_async_remote_copy(
            src_ref=ref, dst_ref=ref, send_sem=ssem, recv_sem=rsem,
            device_id=sibling, device_id_type=MESH,
        ).wait_recv()

    def sent(ref, ssem, rsem):
        pltpu.make_async_remote_copy(
            src_ref=ref, dst_ref=ref, send_sem=ssem, recv_sem=rsem,
            device_id=sibling, device_id_type=MESH,
        ).wait_send()

    load_master = pltpu.make_async_copy(master_hbm, u.at[pl.ds(0, OWN), :], in_sem.at[0])
    load_master.start()
    load_hid = pltpu.make_async_copy(hid_hbm, hid_ref, in_sem.at[1])
    load_hid.start()

    barrier = pltpu.get_barrier_semaphore()

    def greet(o, carry):
        pl.semaphore_signal(barrier, inc=1, device_id={"ed": ed, "ep": peer(o)}, device_id_type=MESH)
        return carry

    lax.fori_loop(1, EXP, greet, 0)
    for dev in (zdev(1), zdev(-1), sibling):
        pl.semaphore_signal(barrier, inc=1, device_id=dev, device_id_type=MESH)

    load_master.wait()
    wts[ed] = u[0:OWN, :].astype(BF)
    pl.semaphore_wait(barrier, EXP - 1 + 3)

    def wpiece(d, k, core, part):
        zo = lax.rem(z - k + NZ, NZ) if d == 0 else lax.rem(z + k, NZ)
        return wts.at[zo * 2 + core, pl.ds(part * WSUB, WSUB), pl.ds(d * HALF, HALF)]

    def w_pass(k, part):
        for d in range(2):
            ref = wpiece(d, k, c, part)
            if k > 0:
                arrived(ref, zw_r.at[d, k - 1, part], zw_s.at[d, k - 1, part])
            if k < NZ - 1:
                send(ref, ref, zw_s.at[d, k, part], zw_r.at[d, k, part], zdev(1 if d == 0 else -1))
        for d in range(2):
            ref = wpiece(d, k, c, part)
            send(ref, ref, sw_s.at[d, k, part], sw_r.at[d, k, part], sibling)

    w_pass(0, 0)

    for q in range(4):
        cols = pl.ds(q * 1024, 1024)
        wide = go_ref[:, cols].astype(F32)
        tok[ep, :, cols] = jnp.concatenate([wide, jnp.zeros((ROWS - TOK, 1024), F32)], axis=0).astype(BF)

    streams = (("x", 1), ("x", -1), ("y", 1), ("y", -1))

    def block_of(q, da, db):
        first, sign = streams[q]
        a, b = (x, y) if first == "x" else (y, x)
        a = lax.rem(a - sign * da + SIDE, SIDE)
        b = lax.rem(b - sign * db + SIDE, SIDE)
        return a * SIDE + b if first == "x" else b * SIDE + a

    def piece(q, da, db):
        return tok.at[block_of(q, da, db), pl.ds(q * 16, 16), :]

    def line_dev(q, phase):
        first, sign = streams[q]
        along_x = (first == "x") == (phase == 1)
        nx = lax.rem(x + sign + SIDE, SIDE) if along_x else x
        ny = y if along_x else lax.rem(y + sign + SIDE, SIDE)
        return {"ed": ed, "ep": nx * SIDE + ny}

    def xy_send1(q, j):
        ref = piece(q, j, 0)
        send(ref, ref, xy_s.at[q, j], xy_r.at[q, j], line_dev(q, 1))

    def xy_send2(q, j, i):
        m = 3 + 4 * j + i
        ref = piece(q, i, j)
        send(ref, ref, xy_s.at[q, m], xy_r.at[q, m], line_dev(q, 2))

    def xy_step(n):
        for q in range(4):
            if n < 3:
                arrived(piece(q, n + 1, 0), xy_r.at[q, n], xy_s.at[q, n])
                if n < 2:
                    xy_send1(q, n + 1)
                xy_send2(q, 0, n + 1)
            else:
                j, i = (n - 3) // 4, (n - 3) % 4
                arrived(piece(q, i, j + 1), xy_r.at[q, n], xy_s.at[q, n])
                if j < 2:
                    xy_send2(q, j + 1, i)

    for q in range(4):
        xy_send1(q, 0)
    for q in range(4):
        xy_send2(q, 0, 0)

    w_pass(0, 1)

    expert_row = lax.broadcasted_iota(I32, (EXP, TOK), 0)
    dense = jnp.zeros((EXP, TOK), F32)
    named = jnp.zeros((EXP, TOK), F32)
    for k in range(routes_ref.shape[0]):
        hit = routes_ref[k : k + 1, :] == expert_row
        dense = dense + jnp.where(hit, gates_ref[k : k + 1, :].astype(F32), 0.0)
        named = named + jnp.where(hit, 1.0, 0.0)
    tile[...] = jnp.zeros_like(tile)
    tile[0:EXP, 0:TOK] = dense
    tile[EXP : 2 * EXP, 0:TOK] = named
    table = jnp.transpose(tile[...])[0:ROWS, :]
    earlier = jnp.where(
        lax.broadcasted_iota(I32, (ROWS, ROWS), 1) < lax.broadcasted_iota(I32, (ROWS, ROWS), 0), 1.0, 0.0
    ).astype(BF)
    lane = lax.broadcasted_iota(I32, (ROWS, 128), 1)
    slot = dot(earlier, table.astype(BF))
    slot = jnp.where(table > 0.5, slot, -1.0)
    gd[ep] = jnp.where((lane >= EXP) & (lane < 2 * EXP), slot, table).astype(BF)


    def gd_send(o, carry):
        send(gd.at[ep], gd.at[ep], gd_s.at[o], gd_r.at[o], {"ed": ed, "ep": peer(o)})
        return carry

    lax.fori_loop(1, EXP, gd_send, 0)

    def gd_wait(o, carry):
        arrived(gd.at[peer(EXP - o)], gd_r.at[o], gd_s.at[o])
        return carry

    u[...] = jnp.zeros_like(u)
    prob[...] = jnp.zeros_like(prob)

    def choose(r):
        rows = pl.ds(r * 256, 256)
        mine = gd[4 * r : 4 * r + 4].reshape(256, 128).astype(F32)
        lanes = lax.broadcasted_iota(I32, (256, 128), 1)
        gate = jnp.sum(jnp.where(lanes == ep, mine, 0.0), axis=1, keepdims=True)
        place = jnp.sum(jnp.where(lanes == EXP + ep, mine, 0.0), axis=1, keepdims=True)
        source = (lax.broadcasted_iota(I32, (256, 1), 0) // ROWS + 4 * r).astype(F32)
        target = jnp.where(place >= 0.0, place * EXP + source, -1.0)
        gatec[rows, :] = jnp.broadcast_to(gate, (256, 128))
        turned = jnp.transpose(jnp.where(lanes == 0, target, jnp.where(lanes == 1, gate, 0.0)))
        slots_down = lax.broadcasted_iota(I32, (SLOTS, 256), 0).astype(F32)
        same = slots_down == turned[0:1, :]
        sel_t[:, rows] = jnp.where(same, 1.0, 0.0).astype(BF)
        gated = jnp.where(same, turned[1:2, :], 0.0).astype(BF)
        for f in range(3):
            cols = pl.ds(f * 512, 512)
            hg_t[cols, rows] = lax.dot_general(
                hid_ref[:, cols], gated, (((0,), (0,)), ((), ())), preferred_element_type=F32
            ).astype(BF)
        slots_across = lax.broadcasted_iota(I32, (256, SLOTS), 1).astype(F32)
        picked = jnp.where(slots_across == target, 1.0, 0.0).astype(BF)
        for f in range(3):
            cols = pl.ds(f * 512, 512)
            h_tok[rows, cols] = dot(picked, hid_ref[:, cols]).astype(BF)

    def p_compute(k, settled):
        place = lax.rem(k, 2)
        for d in range(2):
            zo = lax.rem(z - 1 - k + 2 * NZ, NZ) if d == 0 else lax.rem(z + 1 + k, NZ)

            def side(core):
                cols = pl.ds(pl.multiple_of((zo * 2 + core) * OWN, OWN), OWN)
                return tok[:, :, cols].reshape(ALL, OWN)

            if settled:
                sent(stage.at[d, place], ps_s.at[d, k - 2], ps_r.at[d, k - 2])
            for part in range(NSUB):
                rows = pl.ds(part * RSUB, RSUB)
                stage[d, place, rows, :] = dot(hg_t[pl.ds(d * HALF + part * RSUB, RSUB), :], side(1 - c)).astype(BF)
            send(stage.at[d, place], psib.at[d, k], ps_s.at[d, k], ps_r.at[d, k], sibling)
            for part in range(NSUB):
                rows = pl.ds(part * RSUB, RSUB)
                pown[d, place, rows, :] = dot(hg_t[pl.ds(d * HALF + part * RSUB, RSUB), :], side(c)).astype(BF)

    def rs_part(k, part, first):
        place = lax.rem(k, 2)
        rows = pl.ds(part * RSUB, RSUB)
        for d in range(2):
            if part == 0:
                arrived(psib.at[d, k], ps_r.at[d, k], ps_s.at[d, k])
            total = pown[d, place, rows, :].astype(F32) + psib[d, k, rows, :].astype(F32)
            here = rsb.at[d, k, rows, :]
            if not first:
                arrived(here, rs_r.at[d, k - 1, part], rs_s.at[d, k - 1, part])
                total = total + here[...].astype(F32)
            here[...] = total.astype(BF)
            send(
                here, rsb.at[d, k + 1, rows, :],
                rs_s.at[d, k, part], rs_r.at[d, k, part], zdev(1 if d == 0 else -1),
            )

    def up_step(k, carry):
        for d in range(2):
            zo = lax.rem(z - k + NZ, NZ) if d == 0 else lax.rem(z + k, NZ)
            deep = pl.ds(pl.multiple_of(zo * 512, 512), 512)
            for f in range(HALF // COL):
                cols = pl.ds(d * HALF + f * COL, COL)
                t = tok[:, :, deep].reshape(ALL, 512)
                u[:, cols] += dot(t, wts[pl.ds(zo * 2, 2), :, cols].reshape(512, COL))
        return carry

    def gh_copy(n):
        return pltpu.make_async_copy(
            gh_part.at[n % 2], gh_hbm.at[:, pl.ds(n * COL, COL)], gh_sem.at[n % 2]
        )

    def finish(n):
        cols = pl.ds(n * COL, COL)

        def some(r, carry):
            rows = pl.ds(pl.multiple_of(r * 256, 256), 256)
            up = u[rows, cols]
            prod = up * h_tok[rows, cols].astype(F32)
            prob[rows, :] += prod[:, 0:128] + prod[:, 128:256]
            gate = gatec[rows, :]
            gmul[rows, :] = (jnp.concatenate([gate, gate], axis=1) * up).astype(BF)
            return carry

        lax.fori_loop(0, ALL // 256, some, 0)
        if n >= 2:
            gh_copy(n - 2).wait()
        gh_part[n % 2] = dot(sel_t[...], gmul[...]).astype(BF)
        gh_copy(n).start()

    def sw_wait(k):
        for d in range(2):
            for part in range(NSUB):
                arrived(wpiece(d, k, 1 - c, part), sw_r.at[d, k, part], sw_s.at[d, k, part])

    due = [(XY_PACE * (n + 1), 0, n) for n in range(15)]
    due = due + [(8.0 / NSUB * (NSUB * k + part + 1) - 8.0, 1, k, part) for k in range(1, NZ) for part in range(NSUB)]
    selected, moved, seen = 0, False, 0
    after = 0
    for event in sorted(due):
        if event[1] == 0:
            xy_step(event[2])
            if event[2] == 14:
                p_compute(0, False)
                moved = True
        else:
            w_pass(event[2], event[3])
            if moved:
                after = after + 1
                if after == 1:
                    p_compute(1, False)
                if after == 2:
                    rs_part(0, 0, True)
                    sw_wait(0)
                    up_step(0, 0)
                    rs_part(0, 1, True)
                if after == 3:
                    sw_wait(1)
                    up_step(1, 0)
        seen = seen + 1
        if seen == 3:
            lax.fori_loop(1, EXP, gd_wait, 0)
            load_hid.wait()
        if seen >= 3 and selected < 4:
            choose(selected)
            selected = selected + 1
    for k in range(2, NZ):
        sw_wait(k)

    def early(k, carry):
        p_compute(k + 1, True)
        for part in range(NSUB):
            rs_part(k, part, False)
            up_step(NSUB * (k - 1) + part + 2, 0)
        return carry

    lax.fori_loop(1, 4, early, 0)
    for k in range(4, 6):
        p_compute(k + 1, True)
        for part in range(NSUB):
            rs_part(k, part, False)
            finish(3 * (k - 4) + part)
        finish(3 * (k - 4) + 2)

    for r in range(4):
        rows = pl.ds(r * 256, 256)
        prob[rows, :] = jnp.broadcast_to(jnp.sum(prob[rows, :], axis=1, keepdims=True), (256, 128))

    def prob_at(s):
        return prob.at[pl.ds(pl.multiple_of(s * ROWS, ROWS), ROWS), :]

    def pr_send(o, carry):
        send(prob_at(peer(o)), probr.at[ep], pr_s.at[o], pr_r.at[o], {"ed": ed, "ep": peer(o)})
        return carry

    lax.fori_loop(1, EXP, pr_send, 0)
    probr[ep] = prob[pl.ds(pl.multiple_of(ep * ROWS, ROWS), ROWS), :]

    p_compute(NZ - 1, True)
    for part in range(NSUB):
        rs_part(NZ - 2, part, False)

    for q in range(4):
        for n in range(15):
            da, db = (n, 0) if n < 3 else ((n - 3) % 4, (n - 3) // 4)
            sent(piece(q, da, db), xy_s.at[q, n], xy_r.at[q, n])
    for d in range(2):
        for k in range(NZ):
            for part in range(NSUB):
                ref = wpiece(d, k, c, part)
                if k < NZ - 1:
                    sent(ref, zw_s.at[d, k, part], zw_r.at[d, k, part])
                sent(ref, sw_s.at[d, k, part], sw_r.at[d, k, part])
                if k < NZ - 2:
                    here = rsb.at[d, k, pl.ds(part * RSUB, RSUB), :]
                    sent(here, rs_s.at[d, k, part], rs_r.at[d, k, part])

    def last(o, carry):
        sent(gd.at[ep], gd_s.at[o], gd_r.at[o])
        return carry

    lax.fori_loop(1, EXP, last, 0)
    gh_copy(4).wait()
    gh_copy(5).wait()

    def pr_wait(o, carry):
        arrived(probr.at[peer(EXP - o)], pr_r.at[o], pr_s.at[o])
        return carry

    lax.fori_loop(1, EXP, pr_wait, 0)
    lanes = lax.broadcasted_iota(I32, (ROWS, 128), 1)
    spread = jnp.zeros((ROWS, 128), F32)
    for e in range(EXP):
        spread = jnp.where(lanes == e, probr[e], spread)
    tile[0:ROWS, :] = spread
    turned = jnp.transpose(tile[...])
    picked = jnp.zeros((routes_ref.shape[0], TOK), F32)
    for e in range(EXP):
        picked = picked + jnp.where(routes_ref[...] == e, turned[e : e + 1, 0:TOK], 0.0)
    gg_ref[...] = picked

    def grad_copy(d, part):
        cols = pl.ds(d * HALF + part * RSUB, RSUB)
        return pltpu.make_async_copy(u.at[pl.ds(0, OWN), cols], grad_hbm.at[:, cols], grad_sem.at[d, part])

    for part in range(NSUB):
        rows = pl.ds(part * RSUB, RSUB)
        for d in range(2):
            if part == 0:
                arrived(psib.at[d, NZ - 1], ps_r.at[d, NZ - 1], ps_s.at[d, NZ - 1])
            total = pown[d, (NZ - 1) % 2, rows, :].astype(F32) + psib[d, NZ - 1, rows, :].astype(F32)
            here = rsb.at[d, NZ - 1, rows, :]
            arrived(here, rs_r.at[d, NZ - 2, part], rs_s.at[d, NZ - 2, part])
            total = total + here[...].astype(F32)
            u[0:OWN, d * HALF + part * RSUB : d * HALF + (part + 1) * RSUB] = jnp.transpose(total)
            grad_copy(d, part).start()

    for d in range(2):
        for part in range(NSUB):
            here = rsb.at[d, NZ - 2, pl.ds(part * RSUB, RSUB), :]
            sent(here, rs_s.at[d, NZ - 2, part], rs_r.at[d, NZ - 2, part])
        for k in range(NZ - 2, NZ):
            sent(stage.at[d, k % 2], ps_s.at[d, k], ps_r.at[d, k])

    def pr_last(o, carry):
        sent(prob_at(peer(o)), pr_s.at[o], pr_r.at[o])
        return carry

    lax.fori_loop(1, EXP, pr_last, 0)
    for d in range(2):
        for part in range(NSUB):
            grad_copy(d, part).wait()


def local(grad_out, routes, gates, hidden, master, moment_one, moment_two):
    saved = jnp.transpose(hidden, (0, 2, 3, 1, 4)).reshape(SLOTS, HID)
    own = master.reshape(OWN, HID)
    vmem = pl.BlockSpec(memory_space=pltpu.VMEM)
    dma = pltpu.SemaphoreType.DMA
    gh, gradient, gg = pl.pallas_call(
        body,
        out_shape=(
            jax.ShapeDtypeStruct((SLOTS, HID), BF),
            jax.ShapeDtypeStruct((OWN, HID), F32),
            jax.ShapeDtypeStruct((routes.shape[1], TOK), F32),
        ),
        in_specs=[vmem] * 3 + [pl.BlockSpec(memory_space=pl.ANY)] * 2,
        out_specs=(pl.BlockSpec(memory_space=pl.ANY),) * 2 + (vmem,),
        scratch_shapes=[
            pltpu.VMEM((EXP, ROWS, WIDTH), BF),
            pltpu.VMEM((EXP, OWN, HID), BF),
            pltpu.VMEM((EXP, ROWS, 128), BF),
            pltpu.VMEM((128, 128), F32),
            pltpu.VMEM((ALL, 128), F32),
            pltpu.VMEM((SLOTS, ALL), BF),
            pltpu.VMEM((ALL, HID), BF),
            pltpu.VMEM((HID, ALL), BF),
            pltpu.VMEM((ALL, HID), F32),
            pltpu.VMEM((ALL, COL), BF),
            pltpu.VMEM((SLOTS, HID), BF),
            pltpu.VMEM((2, SLOTS, COL), BF),
            pltpu.VMEM((2, 2, HALF, OWN), BF),
            pltpu.VMEM((2, 2, HALF, OWN), BF),
            pltpu.VMEM((2, NZ, HALF, OWN), BF),
            pltpu.VMEM((2, NZ, HALF, OWN), BF),
            pltpu.VMEM((ALL, 128), F32),
            pltpu.VMEM((EXP, ROWS, 128), F32),
            dma((4, 15)), dma((4, 15)),
            dma((2, NZ - 1, NSUB)), dma((2, NZ - 1, NSUB)),
            dma((2, NZ, NSUB)), dma((2, NZ, NSUB)),
            dma((EXP,)), dma((EXP,)),
            dma((2, NZ)), dma((2, NZ)),
            dma((2, NZ - 1, NSUB)), dma((2, NZ - 1, NSUB)),
            dma((EXP,)), dma((EXP,)),
            dma((2,)), dma((2,)), dma((2, NSUB)),
        ],
        compiler_params=pltpu.CompilerParams(
            collective_id=0, has_side_effects=True, vmem_limit_bytes=LIMIT * 1024 * 1024
        ),
        cost_estimate=pl.CostEstimate(flops=25_000_000_000, bytes_accessed=8_000_000, transcendentals=0),
        name="expert_backward",
    )(grad_out, routes.T, gates.T, saved, own)

    gradient = gradient.reshape(master.shape)
    new_moment_one = beta_first * moment_one + (1.0 - beta_first) * gradient
    new_moment_two = beta_second * moment_two + (1.0 - beta_second) * gradient * gradient
    first_bias = 1.0 - beta_first**20
    second_bias = 1.0 - beta_second**20
    update = new_moment_one / first_bias / (jnp.sqrt(new_moment_two / second_bias) + adam_eps)
    new_master = master - learn_rate * update
    grad_hidden = jnp.transpose(gh.reshape(1, 1, CAP, EXP, HID), (0, 3, 1, 2, 4))
    return (gg.T, grad_hidden, new_master, new_moment_one, new_moment_two)


def solution(mesh):
    in_specs = (
        P(("ed", "ep"), None),
        P(("ed", "ep"), None),
        P(("ed", "ep"), None),
        P("ed", None, "ep", None, None),
        P("ep", "ed", None),
        P("ep", "ed", None),
        P("ep", "ed", None),
    )
    out_specs = (
        P(("ed", "ep"), None),
        P("ed", None, "ep", None, None),
        P("ep", "ed", None),
        P("ep", "ed", None),
        P("ep", "ed", None),
    )
    return jax.shard_map(local, mesh=mesh, in_specs=in_specs, out_specs=out_specs, check_vma=False)
```

```python
import jax
import jax.numpy as jnp
from jax import lax
from jax.experimental import pallas as pl
from jax.experimental.pallas import tpu as pltpu
from jax.sharding import PartitionSpec as P

beta_first = 0.9
beta_second = 0.95
learn_rate = 0.01
adam_eps = 1e-08

MESH = pl.DeviceIdType.MESH
BF = jnp.bfloat16
F32 = jnp.float32
I32 = jnp.int32

NZ = 8
SIDE = 4
EXP = 16
TOK = 56
ROWS = 64
ALL = EXP * ROWS
WIDTH = 4096
HID = 1536
HALF = HID // 2
CAP = 35
SLOTS = CAP * EXP
OWN = 256
COL = 256
LIMIT = 58
R1 = 2.2
W_DUE = (8, 16, 24, 36, 52, 64, 73)
P_DUE = (27.7, 30.5, 61.5, 67.0)
RS_DUE = (30.0, 46.0, 66.0, 77.0)
UP_DUE = (63.0, 33.0, 37.0, 39.0, 41.0, 69.5, 71.0, 78.0)
SLAB = WIDTH // NZ
PLACE = (7, 1, 3, 5, 6, 4, 2, 0)
NSUB = 2
WSUB = OWN // NSUB
RSUB = HALF // NSUB


def dot(a, b):
    return jnp.dot(a, b, preferred_element_type=F32)


def body(
    go_hbm, routes_ref, gates_ref, hid_hbm, master_hbm,
    gh_hbm, grad_hbm, gg_ref,
    tok, wts, gd, tile, gatec, sel_t, h_tok, hg_t, u, gmul, hid_ref, go_ref, gh_part, pown, stage, psib, rsb, prob, probr,
    xy_s, xy_r, zw_s, zw_r, sw_s, sw_r, gd_s, gd_r, ps_s, ps_r, rs_s, rs_r, pr_s, pr_r, in_sem, gh_sem, grad_sem,
):
    ed = lax.axis_index("ed")
    ep = lax.axis_index("ep")
    z, c = ed // 2, ed % 2
    x, y = ep // SIDE, ep % SIDE

    def zdev(k):
        return {"ed": lax.rem(z + k + NZ, NZ) * 2 + c, "ep": ep}

    sibling = {"ed": z * 2 + 1 - c, "ep": ep}

    def peer(o):
        return lax.rem(ep + o, EXP)

    def send(src, dst, ssem, rsem, dev):
        copy = pltpu.make_async_remote_copy(
            src_ref=src, dst_ref=dst, send_sem=ssem, recv_sem=rsem,
            device_id=dev, device_id_type=MESH,
        )
        copy.start()

    def arrived(ref, rsem, ssem):
        pltpu.make_async_remote_copy(
            src_ref=ref, dst_ref=ref, send_sem=ssem, recv_sem=rsem,
            device_id=sibling, device_id_type=MESH,
        ).wait_recv()

    def sent(ref, ssem, rsem):
        pltpu.make_async_remote_copy(
            src_ref=ref, dst_ref=ref, send_sem=ssem, recv_sem=rsem,
            device_id=sibling, device_id_type=MESH,
        ).wait_send()

    load_master = pltpu.make_async_copy(master_hbm, u.at[pl.ds(0, OWN), :], in_sem.at[0])
    load_master.start()
    load_go = pltpu.make_async_copy(go_hbm, go_ref, in_sem.at[2])
    load_go.start()
    load_hid = pltpu.make_async_copy(hid_hbm, hid_ref, in_sem.at[1])
    load_hid.start()

    barrier = pltpu.get_barrier_semaphore()

    def greet(o, carry):
        pl.semaphore_signal(barrier, inc=1, device_id={"ed": ed, "ep": peer(o)}, device_id_type=MESH)
        return carry

    lax.fori_loop(1, EXP, greet, 0)
    for dev in (zdev(1), zdev(-1), sibling):
        pl.semaphore_signal(barrier, inc=1, device_id=dev, device_id_type=MESH)

    load_master.wait()
    wts[ed] = u[0:OWN, :].astype(BF)
    pl.semaphore_wait(barrier, EXP - 1 + 3)

    def wpiece(off, core, part):
        chip = lax.rem(z + off + NZ, NZ)
        return wts.at[chip * 2 + core, pl.ds(part * WSUB, WSUB), :]

    def w_parts(d, k):
        return (0, 1) if k < 4 else (d,)

    def w_off(d, k):
        return -k if d == 0 else k

    def w_pass(k, part):
        for d in range(2):
            if part in w_parts(d, k):
                ref = wpiece(w_off(d, k), c, part)
                if k > 0:
                    arrived(ref, zw_r.at[d, k - 1, part], zw_s.at[d, k - 1, part])
                if k < 4 and part in w_parts(d, k + 1):
                    send(ref, ref, zw_s.at[d, k, part], zw_r.at[d, k, part], zdev(1 if d == 0 else -1))
        for d in range(2 if k > 0 else 1):
            if part in w_parts(d, k):
                ref = wpiece(w_off(d, k), c, part)
                send(ref, ref, sw_s.at[d, k, part], sw_r.at[d, k, part], sibling)

    def w_half(k):
        for part in range(2):
            w_pass(k, part)

    w_pass(0, 0)

    load_go.wait()
    for off in range(NZ):
        cols = pl.ds(pl.multiple_of(lax.rem(z + off, NZ) * SLAB, SLAB), SLAB)
        wide = go_ref[:, cols].astype(F32)
        tok[PLACE[off], ep] = jnp.concatenate([wide, jnp.zeros((ROWS - TOK, SLAB), F32)], axis=0).astype(BF)

    streams = (("x", 1), ("x", -1), ("y", 1), ("y", -1))

    def block_of(q, da, db):
        first, sign = streams[q]
        a, b = (x, y) if first == "x" else (y, x)
        a = lax.rem(a - sign * da + SIDE, SIDE)
        b = lax.rem(b - sign * db + SIDE, SIDE)
        return a * SIDE + b if first == "x" else b * SIDE + a

    def piece(q, half, da, db):
        return tok.at[pl.ds(half * 4, 4), block_of(q, da, db), pl.ds(q * 16, 16), :]

    def line_dev(q, phase):
        first, sign = streams[q]
        along_x = (first == "x") == (phase == 1)
        nx = lax.rem(x + sign + SIDE, SIDE) if along_x else x
        ny = y if along_x else lax.rem(y + sign + SIDE, SIDE)
        return {"ed": ed, "ep": nx * SIDE + ny}

    def xy_send1(q, half, j):
        ref = piece(q, half, j, 0)
        send(ref, ref, xy_s.at[half, q, j], xy_r.at[half, q, j], line_dev(q, 1))

    def xy_send2(q, half, j, i):
        m = 3 + 4 * j + i
        ref = piece(q, half, i, j)
        send(ref, ref, xy_s.at[half, q, m], xy_r.at[half, q, m], line_dev(q, 2))

    def xy_start(half):
        for q in range(4):
            xy_send1(q, half, 0)
        for q in range(4):
            xy_send2(q, half, 0, 0)

    def xy_step(half, n):
        for q in range(4):
            if n < 3:
                arrived(piece(q, half, n + 1, 0), xy_r.at[half, q, n], xy_s.at[half, q, n])
                if n < 2:
                    xy_send1(q, half, n + 1)
                xy_send2(q, half, 0, n + 1)
            else:
                j, i = (n - 3) // 4, (n - 3) % 4
                arrived(piece(q, half, i, j + 1), xy_r.at[half, q, n], xy_s.at[half, q, n])
                if j < 2:
                    xy_send2(q, half, j + 1, i)

    xy_start(0)

    w_pass(0, 1)

    expert_row = lax.broadcasted_iota(I32, (EXP, TOK), 0)
    dense = jnp.zeros((EXP, TOK), F32)
    named = jnp.zeros((EXP, TOK), F32)
    for k in range(routes_ref.shape[0]):
        hit = routes_ref[k : k + 1, :] == expert_row
        dense = dense + jnp.where(hit, gates_ref[k : k + 1, :].astype(F32), 0.0)
        named = named + jnp.where(hit, 1.0, 0.0)
    tile[...] = jnp.zeros_like(tile)
    tile[0:EXP, 0:TOK] = dense
    tile[EXP : 2 * EXP, 0:TOK] = named
    table = jnp.transpose(tile[...])[0:ROWS, :]
    earlier = jnp.where(
        lax.broadcasted_iota(I32, (ROWS, ROWS), 1) < lax.broadcasted_iota(I32, (ROWS, ROWS), 0), 1.0, 0.0
    ).astype(BF)
    lane = lax.broadcasted_iota(I32, (ROWS, 128), 1)
    slot = dot(earlier, table.astype(BF))
    slot = jnp.where(table > 0.5, slot, -1.0)
    gd[ep] = jnp.where((lane >= EXP) & (lane < 2 * EXP), slot, table).astype(BF)


    def gd_send(o, carry):
        send(gd.at[ep], gd.at[ep], gd_s.at[o], gd_r.at[o], {"ed": ed, "ep": peer(o)})
        return carry

    lax.fori_loop(1, EXP, gd_send, 0)

    def gd_wait(o, carry):
        arrived(gd.at[peer(EXP - o)], gd_r.at[o], gd_s.at[o])
        return carry

    u[...] = jnp.zeros_like(u)
    prob[...] = jnp.zeros_like(prob)

    def choose(r):
        rows = pl.ds(r * 256, 256)
        mine = gd[4 * r : 4 * r + 4].reshape(256, 128).astype(F32)
        lanes = lax.broadcasted_iota(I32, (256, 128), 1)
        gate = jnp.sum(jnp.where(lanes == ep, mine, 0.0), axis=1, keepdims=True)
        place = jnp.sum(jnp.where(lanes == EXP + ep, mine, 0.0), axis=1, keepdims=True)
        source = (lax.broadcasted_iota(I32, (256, 1), 0) // ROWS + 4 * r).astype(F32)
        target = jnp.where(place >= 0.0, place * EXP + source, -1.0)
        gatec[rows, :] = jnp.broadcast_to(gate, (256, 128))
        turned = jnp.transpose(jnp.where(lanes == 0, target, jnp.where(lanes == 1, gate, 0.0)))
        slots_down = lax.broadcasted_iota(I32, (SLOTS, 256), 0).astype(F32)
        same = slots_down == turned[0:1, :]
        sel_t[:, rows] = jnp.where(same, 1.0, 0.0).astype(BF)
        gated = jnp.where(same, turned[1:2, :], 0.0).astype(BF)
        for f in range(3):
            cols = pl.ds(f * 512, 512)
            hg_t[cols, rows] = lax.dot_general(
                hid_ref[:, cols], gated, (((0,), (0,)), ((), ())), preferred_element_type=F32
            ).astype(BF)
        slots_across = lax.broadcasted_iota(I32, (256, SLOTS), 1).astype(F32)
        picked = jnp.where(slots_across == target, 1.0, 0.0).astype(BF)
        for f in range(3):
            cols = pl.ds(f * 512, 512)
            h_tok[rows, cols] = dot(picked, hid_ref[:, cols]).astype(BF)

    def p_compute(k):
        place = k % 2
        for d in range(2):
            slab = PLACE[(-1 - k) % NZ if d == 0 else (1 + k) % NZ]

            def side(core):
                cols = pl.ds(pl.multiple_of(core * OWN, OWN), OWN)
                return tok[slab, :, :, cols].reshape(ALL, OWN)

            if k >= 2:
                sent(stage.at[d, place], ps_s.at[d, k - 2], ps_r.at[d, k - 2])
            for part in range(NSUB):
                rows = pl.ds(part * RSUB, RSUB)
                stage[d, place, rows, :] = dot(hg_t[pl.ds(d * HALF + part * RSUB, RSUB), :], side(1 - c)).astype(BF)
            send(stage.at[d, place], psib.at[d, k], ps_s.at[d, k], ps_r.at[d, k], sibling)
            for part in range(NSUB):
                rows = pl.ds(part * RSUB, RSUB)
                pown[d, place, rows, :] = dot(hg_t[pl.ds(d * HALF + part * RSUB, RSUB), :], side(c)).astype(BF)

    def rs_part(k, part):
        place = k % 2
        rows = pl.ds(part * RSUB, RSUB)
        for d in range(2):
            if part == 0:
                arrived(psib.at[d, k], ps_r.at[d, k], ps_s.at[d, k])
            total = pown[d, place, rows, :].astype(F32) + psib[d, k, rows, :].astype(F32)
            here = rsb.at[d, k, rows, :]
            if k > 0:
                arrived(here, rs_r.at[d, k - 1, part], rs_s.at[d, k - 1, part])
                total = total + here[...].astype(F32)
            here[...] = total.astype(BF)
            send(
                here, rsb.at[d, k + 1, rows, :],
                rs_s.at[d, k, part], rs_r.at[d, k, part], zdev(1 if d == 0 else -1),
            )

    def sw_wait(off):
        k = abs(off)
        for d in range(2 if k == 4 else 1):
            d = d if k == 4 else int(off > 0)
            for part in w_parts(d, k):
                arrived(wpiece(off, 1 - c, part), sw_r.at[d, k, part], sw_s.at[d, k, part])

    def up_step(off):
        sw_wait(off)
        chip = lax.rem(z + off + NZ, NZ)
        for f in range(HID // COL):
            cols = pl.ds(f * COL, COL)
            t = tok[PLACE[off % NZ]].reshape(ALL, SLAB)
            u[:, cols] += dot(t, wts[pl.ds(chip * 2, 2), :, cols].reshape(SLAB, COL))

    def gh_copy(n):
        return pltpu.make_async_copy(
            gh_part.at[n % 2], gh_hbm.at[:, pl.ds(n * COL, COL)], gh_sem.at[n % 2]
        )

    def finish(n):
        cols = pl.ds(n * COL, COL)

        def some(r, carry):
            rows = pl.ds(pl.multiple_of(r * 256, 256), 256)
            up = u[rows, cols]
            prod = up * h_tok[rows, cols].astype(F32)
            prob[rows, :] += prod[:, 0:128] + prod[:, 128:256]
            gate = gatec[rows, :]
            gmul[rows, :] = (jnp.concatenate([gate, gate], axis=1) * up).astype(BF)
            return carry

        lax.fori_loop(0, ALL // 256, some, 0)
        if n >= 2:
            gh_copy(n - 2).wait()
        gh_part[n % 2] = dot(sel_t[...], gmul[...]).astype(BF)
        gh_copy(n).start()

    plan = [(1.84 * (n + 1), xy_step, (0, n)) for n in range(15)]
    plan = plan + [(18.0, xy_start, (1,))]
    plan = plan + [(28.0 + R1 * (n + 1), xy_step, (1, n)) for n in range(15)]
    for n in range(6):
        plan = plan + [(W_DUE[n], w_pass, (1 + n // 2, n % 2))]
    plan = plan + [(W_DUE[6], w_half, (4,))]
    for k in range(4):
        plan = plan + [(P_DUE[k], p_compute, (k,)), (RS_DUE[k], rs_part, (k, 0)), (RS_DUE[k] + 2.0, rs_part, (k, 1))]
    plan = plan + [(UP_DUE[n], up_step, ((0, -1, 1, -2, 2, -3, 3, 4)[n],)) for n in range(NZ)]
    plan = plan + [(RS_DUE[3] + 3.0, p_compute, (4,))]
    selected, seen = 0, 0
    for due, act, what in sorted(plan, key=lambda entry: entry[0]):
        act(*what)
        seen = seen + 1
        if seen == 4:
            lax.fori_loop(1, EXP, gd_wait, 0)
            load_hid.wait()
        if seen >= 4 and selected < 4 and seen % 2 == 0:
            choose(selected)
            selected = selected + 1

    for k in range(4, 6):
        p_compute(k + 1)
        rs_part(k, 0)
        finish(3 * (k - 4))
        rs_part(k, 1)
        finish(3 * (k - 4) + 1)
        finish(3 * (k - 4) + 2)

    for r in range(4):
        rows = pl.ds(r * 256, 256)
        prob[rows, :] = jnp.broadcast_to(jnp.sum(prob[rows, :], axis=1, keepdims=True), (256, 128))

    def prob_at(s):
        return prob.at[pl.ds(pl.multiple_of(s * ROWS, ROWS), ROWS), :]

    def pr_send(o, carry):
        send(prob_at(peer(o)), probr.at[ep], pr_s.at[o], pr_r.at[o], {"ed": ed, "ep": peer(o)})
        return carry

    lax.fori_loop(1, EXP, pr_send, 0)
    probr[ep] = prob[pl.ds(pl.multiple_of(ep * ROWS, ROWS), ROWS), :]

    p_compute(NZ - 1)
    for part in range(NSUB):
        rs_part(NZ - 2, part)

    for q in range(4):
        for n in range(15):
            da, db = (n, 0) if n < 3 else ((n - 3) % 4, (n - 3) // 4)
            for half in range(2):
                sent(piece(q, half, da, db), xy_s.at[half, q, n], xy_r.at[half, q, n])
    for d in range(2):
        for k in range(NZ):
            for part in range(NSUB):
                if k < 5 and part in w_parts(d, k):
                    ref = wpiece(w_off(d, k), c, part)
                    if k < 4 and part in w_parts(d, k + 1):
                        sent(ref, zw_s.at[d, k, part], zw_r.at[d, k, part])
                    if k > 0 or d == 0:
                        sent(ref, sw_s.at[d, k, part], sw_r.at[d, k, part])
                if k < NZ - 2:
                    here = rsb.at[d, k, pl.ds(part * RSUB, RSUB), :]
                    sent(here, rs_s.at[d, k, part], rs_r.at[d, k, part])

    def last(o, carry):
        sent(gd.at[ep], gd_s.at[o], gd_r.at[o])
        return carry

    lax.fori_loop(1, EXP, last, 0)
    gh_copy(4).wait()
    gh_copy(5).wait()

    def pr_wait(o, carry):
        arrived(probr.at[peer(EXP - o)], pr_r.at[o], pr_s.at[o])
        return carry

    lax.fori_loop(1, EXP, pr_wait, 0)
    lanes = lax.broadcasted_iota(I32, (ROWS, 128), 1)
    spread = jnp.zeros((ROWS, 128), F32)
    for e in range(EXP):
        spread = jnp.where(lanes == e, probr[e], spread)
    tile[0:ROWS, :] = spread
    turned = jnp.transpose(tile[...])
    picked = jnp.zeros((routes_ref.shape[0], TOK), F32)
    for e in range(EXP):
        picked = picked + jnp.where(routes_ref[...] == e, turned[e : e + 1, 0:TOK], 0.0)
    gg_ref[...] = picked

    def grad_copy(d, part):
        cols = pl.ds(d * HALF + part * RSUB, RSUB)
        return pltpu.make_async_copy(u.at[pl.ds(0, OWN), cols], grad_hbm.at[:, cols], grad_sem.at[d, part])

    for part in range(NSUB):
        rows = pl.ds(part * RSUB, RSUB)
        for d in range(2):
            if part == 0:
                arrived(psib.at[d, NZ - 1], ps_r.at[d, NZ - 1], ps_s.at[d, NZ - 1])
            total = pown[d, (NZ - 1) % 2, rows, :].astype(F32) + psib[d, NZ - 1, rows, :].astype(F32)
            here = rsb.at[d, NZ - 1, rows, :]
            arrived(here, rs_r.at[d, NZ - 2, part], rs_s.at[d, NZ - 2, part])
            total = total + here[...].astype(F32)
            u[0:OWN, d * HALF + part * RSUB : d * HALF + (part + 1) * RSUB] = jnp.transpose(total)
            grad_copy(d, part).start()

    for d in range(2):
        for part in range(NSUB):
            here = rsb.at[d, NZ - 2, pl.ds(part * RSUB, RSUB), :]
            sent(here, rs_s.at[d, NZ - 2, part], rs_r.at[d, NZ - 2, part])
        for k in range(NZ - 2, NZ):
            sent(stage.at[d, k % 2], ps_s.at[d, k], ps_r.at[d, k])

    def pr_last(o, carry):
        sent(prob_at(peer(o)), pr_s.at[o], pr_r.at[o])
        return carry

    lax.fori_loop(1, EXP, pr_last, 0)
    for d in range(2):
        for part in range(NSUB):
            grad_copy(d, part).wait()


def local(grad_out, routes, gates, hidden, master, moment_one, moment_two):
    saved = jnp.transpose(hidden, (0, 2, 3, 1, 4)).reshape(SLOTS, HID)
    own = master.reshape(OWN, HID)
    vmem = pl.BlockSpec(memory_space=pltpu.VMEM)
    anywhere = pl.BlockSpec(memory_space=pl.ANY)
    dma = pltpu.SemaphoreType.DMA
    gh, gradient, gg = pl.pallas_call(
        body,
        out_shape=(
            jax.ShapeDtypeStruct((SLOTS, HID), BF),
            jax.ShapeDtypeStruct((OWN, HID), F32),
            jax.ShapeDtypeStruct((routes.shape[1], TOK), F32),
        ),
        in_specs=[anywhere, vmem, vmem, anywhere, anywhere],
        out_specs=(anywhere, anywhere, vmem),
        scratch_shapes=[
            pltpu.VMEM((NZ, EXP, ROWS, SLAB), BF),
            pltpu.VMEM((EXP, OWN, HID), BF),
            pltpu.VMEM((EXP, ROWS, 128), BF),
            pltpu.VMEM((128, 128), F32),
            pltpu.VMEM((ALL, 128), F32),
            pltpu.VMEM((SLOTS, ALL), BF),
            pltpu.VMEM((ALL, HID), BF),
            pltpu.VMEM((HID, ALL), BF),
            pltpu.VMEM((ALL, HID), F32),
            pltpu.VMEM((ALL, COL), BF),
            pltpu.VMEM((SLOTS, HID), BF),
            pltpu.VMEM((TOK, WIDTH), BF),
            pltpu.VMEM((2, SLOTS, COL), BF),
            pltpu.VMEM((2, 2, HALF, OWN), BF),
            pltpu.VMEM((2, 2, HALF, OWN), BF),
            pltpu.VMEM((2, NZ, HALF, OWN), BF),
            pltpu.VMEM((2, NZ, HALF, OWN), BF),
            pltpu.VMEM((ALL, 128), F32),
            pltpu.VMEM((EXP, ROWS, 128), F32),
            dma((2, 4, 15)), dma((2, 4, 15)),
            dma((2, 4, NSUB)), dma((2, 4, NSUB)),
            dma((2, 5, NSUB)), dma((2, 5, NSUB)),
            dma((EXP,)), dma((EXP,)),
            dma((2, NZ)), dma((2, NZ)),
            dma((2, NZ - 1, NSUB)), dma((2, NZ - 1, NSUB)),
            dma((EXP,)), dma((EXP,)),
            dma((3,)), dma((2,)), dma((2, NSUB)),
        ],
        compiler_params=pltpu.CompilerParams(
            collective_id=0, has_side_effects=True, vmem_limit_bytes=LIMIT * 1024 * 1024
        ),
        cost_estimate=pl.CostEstimate(flops=25_000_000_000, bytes_accessed=8_000_000, transcendentals=0),
        name="expert_backward",
    )(grad_out, routes.T, gates.T, saved, own)

    gradient = gradient.reshape(master.shape)
    new_moment_one = beta_first * moment_one + (1.0 - beta_first) * gradient
    new_moment_two = beta_second * moment_two + (1.0 - beta_second) * gradient * gradient
    first_bias = 1.0 - beta_first**20
    second_bias = 1.0 - beta_second**20
    update = new_moment_one / first_bias / (jnp.sqrt(new_moment_two / second_bias) + adam_eps)
    new_master = master - learn_rate * update
    grad_hidden = jnp.transpose(gh.reshape(1, 1, CAP, EXP, HID), (0, 3, 1, 2, 4))
    return (gg.T, grad_hidden, new_master, new_moment_one, new_moment_two)


def solution(mesh):
    in_specs = (
        P(("ed", "ep"), None),
        P(("ed", "ep"), None),
        P(("ed", "ep"), None),
        P("ed", None, "ep", None, None),
        P("ep", "ed", None),
        P("ep", "ed", None),
        P("ep", "ed", None),
    )
    out_specs = (
        P(("ed", "ep"), None),
        P("ed", None, "ep", None, None),
        P("ep", "ed", None),
        P("ep", "ed", None),
        P("ep", "ed", None),
    )
    return jax.shard_map(local, mesh=mesh, in_specs=in_specs, out_specs=out_specs, check_vma=False)
```
